256 devices in a mesh: dp: 8 (over x, core), row: 8 (over z), col: 4 (over y).
Axes of the slice: x: 4, y: 4, z: 8, core: 2. Of those that a mesh axis runs over, the one named last changes fastest.
Arguments:
- tokens: bfloat16 [2048, 8192], P('dp', 'row'), may hold values from -0.119628906 to 0.119628906
- upstream: bfloat16 [2048, 14848], P('dp', 'col'), may hold values from -6 to 6
- weight: bfloat16 [8192, 14848], P('row', 'col'), may hold values from -0.0625 to 0.0625
- factor_b: bfloat16 [8192, 32], P('row'), may hold values from -0.0625 to 0.0625
- factor_a: bfloat16 [32, 14848], P(None, 'col'), may hold values from -0.046875 to 0.046875
- magnitude: float32 [14848], P('col'), may hold values from 0.5 to 2
Outputs:
- grad_tokens: bfloat16 [2048, 8192], P('dp', ('row', 'col'))
- grad_magnitude: float32 [14848], P('col')
- grad_a: float32 [32, 14848], P(None, 'col')
- grad_b: float32 [8192, 32], P('row')
The draws below stay inside these ranges and needn't reach their ends.
All inputs are finite; a program needn't handle non-finite values.
Results may differ from the reference program's by a relative error of at most 0.0049.
Values sent between devices are 32-bit elements; how exact they have to be, the bound alone decides.
No kernel may reach another device: no remote copies, remote signals or barrier semaphores. Data moves between devices by JAX's collectives and lax.ppermute only.
A program may use at most 128 MiB of HBM per device.

```python
import math
import jax
import jax.numpy as jnp
from jax import lax

D = 8192
FFW = 14848
RANK = 32
TOK_DEV = 256
TOKENS = 2048
N_DP = 8


def shard_levels(rng, dims, shards, smallest, high):
    def one(dim, blocks):
        steps = jax.random.uniform(jax.random.fold_in(jax.random.fold_in(rng, 6), dim), (blocks,), jnp.float32, smallest / len(shards), high / len(shards))
        return jnp.repeat(jnp.exp(steps), dims[dim] // blocks).reshape((-1,) + (1,) * (len(dims) - dim - 1))

    gain = one(*shards[0])
    for cut in shards[1:]:
        gain = gain * one(*cut)
    return gain


def centred(rng, dims, spread, most, split=(), dtype=jnp.bfloat16):
    entries = jax.random.normal(rng, dims, jnp.float32) * spread
    if len(split) > 0:
        entries = shard_levels(rng, dims, split, -0.22, 0.18) * entries
    return jnp.clip(entries, min=-most, max=most).astype(dtype)


def setup_inputs(seed: int = 0) -> dict:
    streams_of = jax.random.split(jax.random.key(seed), 7)
    tokens = centred(streams_of[0], (TOKENS, D), 0.02, 0.119628906, ((0, 8), (1, 8)))
    upstream = centred(streams_of[1], (TOKENS, FFW), 1.0, 6.0, ((0, 8), (1, 4)))
    weight = centred(streams_of[2], (D, FFW), D ** -0.5, 0.0625, ((0, 8), (1, 4)))
    factor_b = centred(streams_of[3], (D, RANK), D ** -0.5, 0.0625, ((0, 8),))
    factor_a = centred(streams_of[4], (RANK, FFW), FFW ** -0.5, 0.046875, ((1, 4),))
    magnitude = jnp.clip(jnp.exp(math.log(2.0) - 1.3862944 * jax.random.uniform(streams_of[5], (FFW,), jnp.float32) ** shard_levels(streams_of[5], (FFW,), ((0, 4),), -0.2, 0.2)), 0.5, 2.0)
    return dict(tokens=tokens, upstream=upstream, weight=weight, factor_b=factor_b, factor_a=factor_a, magnitude=magnitude)


SCALE = 2.0
EPS = 1e-06

def reference(tokens, upstream, weight, factor_b, factor_a, magnitude):
    blocks = 8
    width = FFW // blocks
    w_blocks = weight.reshape(D, blocks, width).transpose(1, 0, 2)
    a_blocks = factor_a.reshape(RANK, blocks, width).transpose(1, 0, 2)
    g_blocks = upstream.reshape(TOKENS, blocks, width).transpose(1, 0, 2)
    m_blocks = magnitude.reshape(blocks, width)
    tok_groups = tokens.reshape(N_DP, TOK_DEV, D)

    def step(carry, item):
        gx_acc, gb_acc = carry
        w_part, a_part, g_part, m_part = item
        merged_raw = w_part.astype(jnp.float32) + SCALE * jnp.dot(factor_b, a_part, preferred_element_type=jnp.float32)
        normsq = lax.optimization_barrier(jnp.sum(merged_raw * merged_raw, 0)) + EPS
        ratio = m_part / jnp.sqrt(normsq)
        merged = (merged_raw * ratio).astype(jnp.bfloat16)
        gx_acc = gx_acc + jnp.dot(g_part, merged.T, preferred_element_type=jnp.float32)
        g_groups = g_part.reshape(N_DP, TOK_DEV, width)
        outers = jnp.einsum('stk,stj->skj', tok_groups.astype(jnp.float32), g_groups.astype(jnp.float32))
        outer = lax.optimization_barrier(jnp.sum(outers, 0))
        along = lax.optimization_barrier(jnp.sum(outer * merged_raw, 0))
        correction = merged_raw * (along / (normsq * N_DP))

        def group_grads(outer_s):
            grad_merged = (ratio * (outer_s - correction)).astype(jnp.bfloat16)
            ga = SCALE * jnp.dot(factor_b.T, grad_merged, preferred_element_type=jnp.float32)
            gb = SCALE * jnp.dot(grad_merged, a_part.T, preferred_element_type=jnp.float32)
            return (ga, gb)
        ga_all, gb_all = lax.map(group_grads, outers)
        gb_acc = gb_acc + lax.optimization_barrier(jnp.sum(gb_all, 0))
        return ((gx_acc, gb_acc), (along / jnp.sqrt(normsq), lax.optimization_barrier(jnp.sum(ga_all, 0))))
    start = (jnp.zeros((TOKENS, D), jnp.float32), jnp.zeros((D, RANK), jnp.float32))
    (gx_acc, gb_acc), (gm_blocks, ga_blocks) = lax.scan(step, start, (w_blocks, a_blocks, g_blocks, m_blocks))
    grad_tokens = gx_acc.astype(jnp.bfloat16)
    grad_magnitude = gm_blocks.reshape(FFW)
    grad_a = ga_blocks.transpose(1, 0, 2).reshape(RANK, FFW)
    return (grad_tokens, grad_magnitude, grad_a, gb_acc)
```

```python
import jax
import jax.numpy as jnp
from jax import lax
from jax.experimental import pallas as pl
from jax.experimental.pallas import tpu as pltpu
from jax.sharding import PartitionSpec as P

SCALE = 2.0
EPS = 1e-06

TOK, ROWS, COLS, RANK = 256, 1024, 3712, 32
CW = 512
NC = 8
WIDTHS = [min(CW, COLS - CW * c) for c in range(NC)]
PW = CW + 128
PH = 40
X_GROUPS = [[0, 2, 4, 6], [1, 3, 5, 7]]
CORE_FLIP = [(i, i ^ 1) for i in range(8)]
F32, BF16 = jnp.float32, jnp.bfloat16
NN = (((1,), (0,)), ((), ()))
NT = (((1,), (1,)), ((), ()))
TN = (((0,), (0,)), ((), ()))

VMEM = pl.BlockSpec(memory_space=pltpu.VMEM)
SMEM = pl.BlockSpec(memory_space=pltpu.SMEM)
HBM = pl.BlockSpec(memory_space=pl.ANY)


def mm(a, b, dims):
    return lax.dot_general(a, b, dims, preferred_element_type=F32)


def span(c):
    return pl.ds(CW * c, WIDTHS[c])


def fetch(w_hbm, u_hbm, w_v, u_v, sems):
    copies = []
    for c in range(NC):
        pair = (
            pltpu.make_async_copy(w_hbm.at[:, span(c)], w_v.at[:, span(c)], sems.at[0, c]),
            pltpu.make_async_copy(u_hbm.at[:, span(c)], u_v.at[:, span(c)], sems.at[1, c]),
        )
        for copy in pair:
            copy.start()
        copies.append(pair)
    return copies


def first_kernel(pos, tok_ref, bt_ref, a_ref, w_hbm, u_hbm, out, w_v, u_v, a_v, sems):
    copies = fetch(w_hbm, u_hbm, w_v, u_v, sems)
    w_v[:, COLS:] = jnp.zeros((ROWS, NC * CW - COLS), BF16)
    a_v[:, :COLS] = a_ref[...]
    a_v[:, COLS:] = jnp.zeros((RANK, NC * CW - COLS), BF16)
    out[NC - 1] = jnp.zeros((8, CW), F32)
    tok, bt = tok_ref[...], bt_ref[...]
    b2t = bt * BF16(SCALE)
    low = mm(bt, tok, NT)
    low2 = mm(tok, b2t, NT).astype(BF16)
    gram = mm(bt, b2t, NT).astype(BF16)
    for r in range(NC):
        for i in range(4):
            lane = TOK * (i % 2)
            out[r, 6 + i // 2 : 7 + i // 2, lane : lane + TOK] = low[4 * r + i : 4 * r + i + 1]
    for c in range(NC):
        for copy in copies[c]:
            copy.wait()
        n = WIDTHS[c]
        wc, ac = w_v[:, span(c)], a_v[:, span(c)]
        merged = wc.astype(F32) + mm(b2t, ac, TN)
        out[c, 0:1, :n] = jnp.sum(merged * merged, 0, keepdims=True)
        y = mm(tok, wc, NN) + mm(low2, ac, NN)
        out[c, 1:2, :n] = jnp.sum(u_v[:, span(c)].astype(F32) * y, 0, keepdims=True)
    mine = pl.ds(pl.multiple_of(pos[0] * CW, CW), CW)
    q = mm(bt, w_v[:, mine], NN) + mm(gram, a_v[:, mine], NN)
    for r in range(NC):
        out[r, 2:6, :] = q[4 * r : 4 * r + 4]


def second_kernel(
    pos, zz, mag, tok_ref, bt_ref, a_ref, w_hbm, u_hbm, keep, send, s_out, w_v, u_v, g_v, t_v, sems
):
    copies = fetch(w_hbm, u_hbm, w_v, u_v, sems)
    tok, bt = tok_ref[...], bt_ref[...]
    b2t = bt * BF16(SCALE)
    for r in range(NC):
        for i in range(4):
            lane = TOK * (i % 2)
            t_v[4 * r + i : 4 * r + i + 1, :] = zz[r, 6 + i // 2 : 7 + i // 2, lane : lane + TOK]
    low = t_v[...]
    high = low.astype(BF16)
    pair = jnp.concatenate([high, (low - high.astype(F32)).astype(BF16)], 0)
    s_sum = jnp.zeros((RANK, TOK), F32)
    va_sum = jnp.zeros((RANK, RANK), F32)
    vm_sum = jnp.zeros((RANK, ROWS), F32)
    g_v[NC - 1] = jnp.zeros((PH, PW), F32)
    for c in range(NC):
        for copy in copies[c]:
            copy.wait()
        n = WIDTHS[c]
        wc, uc, ac = w_v[:, span(c)], u_v[:, span(c)], a_ref[:, span(c)]
        normsq = zz[c, 0:1, :n] + EPS
        along = zz[c, 1:2, :n]
        ratio = mag[c : c + 1, :n] / jnp.sqrt(normsq)
        v = (ac.astype(F32) * (ratio * (along / normsq))).astype(BF16)
        scaled = (uc.astype(F32) * ratio).astype(BF16)
        s_sum = s_sum + mm(ac, scaled, NT)
        va_sum = va_sum + mm(v, ac, NT)
        vm_sum = vm_sum + mm(v, wc, NT)
        p = mm(pair, uc, NN)
        g_v[c, :RANK, :n] = (SCALE * ratio) * (p[:RANK] + p[RANK:])
        g_v[c, RANK : RANK + 1, :n] = along
        g_v[c, RANK + 1 :, :] = jnp.zeros((PH - RANK - 1, PW), F32)
        g_v[c, RANK : RANK + 1, CW:] = jnp.zeros((1, PW - CW), F32)
    s_out[...] = s_sum
    gb = mm(s_sum.astype(BF16), tok, NN) - vm_sum - mm(va_sum.astype(BF16), b2t, NN)
    gb = SCALE * gb
    for c in range(NC):
        g_v[c, :RANK, CW:] = gb[:, 128 * c : 128 * (c + 1)]
    core = pos[1]
    for x in range(4):
        keep[x] = g_v[2 * x + core]
        send[x] = g_v[2 * x + 1 - core]


def third_kernel(
    pos, zz, mag, s_ref, bt_ref, w_hbm, u_hbm, o0, o1, o2, o3, w_v, u_v, acc, sems
):
    copies = fetch(w_hbm, u_hbm, w_v, u_v, sems)
    b2t = bt_ref[...] * BF16(SCALE)
    acc[...] = mm(s_ref[...].astype(BF16), b2t, TN)
    for c in range(NC):
        for copy in copies[c]:
            copy.wait()
        n = WIDTHS[c]
        ratio = mag[c : c + 1, :n] / jnp.sqrt(zz[c, 0:1, :n] + EPS)
        scaled = (u_v[:, span(c)].astype(F32) * ratio).astype(BF16)
        acc[...] += mm(scaled, w_v[:, span(c)], NT)
    for d, o in enumerate((o0, o1, o2, o3)):
        part = lax.rem(pos[2] + d, 4)
        o[...] = acc[:, pl.ds(pl.multiple_of(part * 256, 256), 256)]


def combine_kernel(pos, y, zz, mag, pack, gb4):
    s = pos[0]
    total = (y[0] + y[1]) + (y[2] + y[3])
    mine = zz[s]
    normsq = mine[0:1] + EPS
    root = jnp.sqrt(normsq)
    ratio = mag[pl.ds(s, 1), :] / root
    along = total[RANK : RANK + 1, :CW]
    factor = (SCALE * ratio) * (along / normsq)
    for r in range(NC):
        rows = slice(4 * r, 4 * r + 4)
        pack[rows, :CW] = total[rows, :CW] - factor * zz[r, 2:6, :]
    pack[RANK : RANK + 1, :CW] = along / root
    pack[RANK + 1 :, :CW] = jnp.zeros((PH - RANK - 1, CW), F32)
    pack[:, CW:] = jnp.zeros((PH, PW - CW), F32)
    gb = total[:RANK, CW:]
    for i in range(4):
        gb4[i] = gb


def spread_kernel(pack, gb4, out):
    gb = (gb4[0] + gb4[1]) + (gb4[2] + gb4[3])
    for i in range(4):
        out[i] = pack[...]
        out[i, :RANK, CW:] = gb


def last_kernel(pos, own, other, ga, gm, gb, both):
    core = pos[1]
    for x in range(4):
        both[2 * x + core] = own[x]
        both[2 * x + 1 - core] = other[x]
    for c in range(NC):
        ga[:, span(c)] = both[c, :RANK, : WIDTHS[c]]
        gm[c : c + 1, :] = both[c, RANK : RANK + 1, :CW]
        gb[:, 128 * c : 128 * (c + 1)] = both[c, :RANK, CW:]


def call(kernel, name, ins, outs, scratch=(), cost=None, limit=48):
    shapes = [jax.ShapeDtypeStruct(shape, F32) for shape in outs]
    return pl.pallas_call(
        kernel,
        name=name,
        out_shape=shapes if len(shapes) > 1 else shapes[0],
        in_specs=ins,
        out_specs=[VMEM] * len(outs) if len(outs) > 1 else VMEM,
        scratch_shapes=list(scratch),
        cost_estimate=cost,
        compiler_params=pltpu.CompilerParams(vmem_limit_bytes=limit << 20),
    )


LOADED = (
    pltpu.VMEM((ROWS, COLS), BF16),
    pltpu.VMEM((TOK, COLS), BF16),
)
COST = pl.CostEstimate(
    flops=4 * TOK * ROWS * COLS, bytes_accessed=10_000_000, transcendentals=COLS
)


def shards(tokens, upstream, weight, factor_b, factor_a, magnitude):
    dp = lax.axis_index("dp")
    pos = jnp.stack([dp, lax.rem(dp, 2), lax.axis_index("col")]).astype(jnp.int32)
    bt = factor_b.T
    mag = jnp.pad(magnitude, (0, NC * CW - COLS)).reshape(NC, CW)
    part = call(
        first_kernel,
        "norms",
        [SMEM, VMEM, VMEM, VMEM, HBM, HBM],
        [(NC, 8, CW)],
        (
            pltpu.VMEM((ROWS, NC * CW), BF16),
            pltpu.VMEM((TOK, COLS), BF16),
            pltpu.VMEM((RANK, NC * CW), BF16),
            pltpu.SemaphoreType.DMA((2, NC)),
        ),
        COST,
    )(pos, tokens, bt, factor_a, weight, upstream)
    z = jnp.sum(lax.all_to_all(part, "row", 0, 0, tiled=True), 0)
    zz = lax.all_to_all(jnp.broadcast_to(z[None], part.shape), "row", 0, 0, tiled=True)

    keep, send, s_part = call(
        second_kernel,
        "factors",
        [SMEM, VMEM, VMEM, VMEM, VMEM, VMEM, HBM, HBM],
        [(4, PH, PW), (4, PH, PW), (RANK, TOK)],
        LOADED
        + (
            pltpu.VMEM((NC, PH, PW), F32),
            pltpu.VMEM((RANK, TOK), F32),
            pltpu.SemaphoreType.DMA((2, NC)),
        ),
        COST,
    )(pos, zz, mag, tokens, bt, factor_a, weight, upstream)
    halves = keep + lax.ppermute(send, "dp", CORE_FLIP)
    y = lax.all_to_all(halves, "dp", 0, 0, tiled=True, axis_index_groups=X_GROUPS)

    o0, o1, o2, o3 = call(
        third_kernel,
        "tokens_grad",
        [SMEM, VMEM, VMEM, VMEM, VMEM, HBM, HBM],
        [(TOK, 256)] * 4,
        LOADED + (pltpu.VMEM((TOK, ROWS), F32), pltpu.SemaphoreType.DMA((2, NC))),
        COST,
    )(pos, zz, mag, s_part, bt, weight, upstream)

    pack, gb4 = call(
        combine_kernel, "combine", [SMEM, VMEM, VMEM, VMEM], [(PH, PW), (4, RANK, 128)]
    )(pos, y, zz, mag)
    gb4 = lax.all_to_all(gb4, "col", 0, 0, tiled=True)
    gb4, o1, o2, o3 = lax.optimization_barrier((gb4, o1, o2, o3))
    arrived = [
        lax.ppermute(o, "col", [(i, (i + d) % 4) for i in range(4)])
        for d, o in ((1, o1), (2, o2), (3, o3))
    ]
    packs = call(spread_kernel, "spread", [VMEM, VMEM], [(4, PH, PW)])(pack, gb4)
    own = lax.all_to_all(packs, "dp", 0, 0, tiled=True, axis_index_groups=X_GROUPS)
    other = lax.ppermute(own, "dp", CORE_FLIP)
    grad_a, gm, gbt = call(
        last_kernel,
        "outputs",
        [SMEM, VMEM, VMEM],
        [(RANK, COLS), (NC, CW), (RANK, ROWS)],
        (pltpu.VMEM((NC, PH, PW), F32),),
    )(pos, own, other)
    grad_tokens = ((o0 + arrived[0]) + (arrived[1] + arrived[2])).astype(BF16)
    return grad_tokens, gm.reshape(-1)[:COLS], grad_a, gbt.T


def solution(mesh):
    placed = (
        P("dp", "row"),
        P("dp", "col"),
        P("row", "col"),
        P("row", None),
        P(None, "col"),
        P("col"),
    )
    return jax.shard_map(
        shards,
        mesh=mesh,
        in_specs=placed,
        out_specs=(P("dp", ("row", "col")), P("col"), P(None, "col"), P("row", None)),
        check_vma=False,
    )
```

```python
import jax
import jax.numpy as jnp
from jax import lax
from jax.experimental import pallas as pl
from jax.experimental.pallas import tpu as pltpu
from jax.sharding import PartitionSpec as P

SCALE = 2.0
EPS = 1e-06

TOK, ROWS, COLS, RANK = 256, 1024, 3712, 32
CW = 512
NC = 8
LIMIT = 28
DEPTH = 2
UNITS = [512] * 7 + [128]
WIDTHS = [min(CW, COLS - CW * c) for c in range(NC)]
PW = CW + 128
PH = 40
X_GROUPS = [[0, 2, 4, 6], [1, 3, 5, 7]]
CORE_FLIP = [(i, i ^ 1) for i in range(8)]
F32, BF16 = jnp.float32, jnp.bfloat16
NN = (((1,), (0,)), ((), ()))
NT = (((1,), (1,)), ((), ()))
TN = (((0,), (0,)), ((), ()))

VMEM = pl.BlockSpec(memory_space=pltpu.VMEM)
HBM = pl.BlockSpec(memory_space=pl.ANY)


def mm(a, b, dims):
    return lax.dot_general(a, b, dims, preferred_element_type=F32)


def dp_place():
    return lax.axis_index("dp")


def span(c):
    return pl.ds(CW * c, WIDTHS[c])


def first_kernel(tok_h, bt_h, a_h, w_h, u_h, out, tok, bt, a, u, w, tok_t, b_v, sems, small):
    firsts = [
        pltpu.make_async_copy(src, dst, small.at[i])
        for i, (src, dst) in enumerate(((tok_h, tok), (bt_h, bt), (a_h, a)))
    ]
    for copy in firsts:
        copy.start()
    units = [(sum(UNITS[:i]), n) for i, n in enumerate(UNITS)]
    copies = [
        [
            pltpu.make_async_copy(src.at[:, pl.ds(at, n)], dst.at[:, pl.ds(at, n)], sems.at[j, i])
            for j, (src, dst) in enumerate(((u_h, u), (w_h, w)))
        ]
        for i, (at, n) in enumerate(units)
    ]

    def begin(i):
        if i < len(units):
            copies[i][0].start()
            copies[i][1].start()

    for i in range(DEPTH):
        begin(i)
    out[NC - 1] = jnp.zeros((8, CW), F32)
    for copy in firsts:
        copy.wait()
    b2t = bt[...] * BF16(SCALE)
    tok_t[...] = tok[...].T
    b_v[...] = b2t.T
    low = mm(bt[...], tok[...], NT)
    gram = mm(bt[...], b2t, NT).astype(BF16)
    for r in range(NC):
        for i in range(4):
            lane = TOK * (i % 2)
            out[r, 6 + i // 2 : 7 + i // 2, lane : lane + TOK] = low[4 * r + i : 4 * r + i + 1]
    for i, (at, n) in enumerate(units):
        copies[i][0].wait()
        copies[i][1].wait()
        begin(i + DEPTH)
        here = pl.ds(at, n)
        merged = w[:, here].astype(F32) + mm(b_v[...], a[:, here], NN)
        outer = mm(tok_t[...], u[:, here], NN)
        squares = jnp.sum((merged * merged).reshape(ROWS // 8, 8, n), 0)
        products = jnp.sum((merged * outer).reshape(ROWS // 8, 8, n), 0)
        lo = at % CW
        out[at // CW, 0:1, lo : lo + n] = jnp.sum(squares, 0, keepdims=True)
        out[at // CW, 1:2, lo : lo + n] = jnp.sum(products, 0, keepdims=True)
    last = NC - 1

    def store(q, n):
        for r in range(NC):
            out[r, 2:6, :n] = q[4 * r : 4 * r + 4]
            if n < CW:
                out[r, 2:6, n:] = jnp.zeros((4, CW - n), F32)

    place = dp_place()

    @pl.when(place < last)
    def _():
        mine = pl.ds(pl.multiple_of(place * CW, CW), CW)
        store(mm(bt[...], w[:, mine], NN) + mm(gram, a[:, mine], NN), CW)

    @pl.when(place == last)
    def _():
        store(mm(bt[...], w[:, span(last)], NN) + mm(gram, a[:, span(last)], NN), WIDTHS[last])


def columns(src, dst, sems):
    copies = [
        pltpu.make_async_copy(src.at[:, span(c)], dst.at[:, span(c)], sems.at[c])
        for c in range(NC)
    ]
    for copy in copies:
        copy.start()
    return copies


def second_kernel(zz, mag, tok, bt, a, u, w_h, keep, send, s_out, g_v, t_v, v_v, w, sems):
    copies = columns(w_h, w, sems)
    b2t = bt[...] * BF16(SCALE)
    for r in range(NC):
        for i in range(4):
            lane = TOK * (i % 2)
            t_v[4 * r + i : 4 * r + i + 1, :] = zz[r, 6 + i // 2 : 7 + i // 2, lane : lane + TOK]
    low = t_v[...]
    high = low.astype(BF16)
    pair = jnp.concatenate([high, (low - high.astype(F32)).astype(BF16)], 0)
    s_sum = jnp.zeros((RANK, TOK), F32)
    va_sum = jnp.zeros((RANK, RANK), F32)
    vm_sum = jnp.zeros((RANK, ROWS), F32)
    g_v[NC - 1] = jnp.zeros((PH, PW), F32)
    for c in range(NC):
        n = WIDTHS[c]
        uc, ac = u[:, span(c)], a[:, span(c)]
        normsq = zz[c, 0:1, :n] + EPS
        along = zz[c, 1:2, :n]
        ratio = mag[c : c + 1, :n] / jnp.sqrt(normsq)
        v = (ac.astype(F32) * (ratio * (along / normsq))).astype(BF16)
        scaled = (uc.astype(F32) * ratio).astype(BF16)
        s_sum = s_sum + mm(ac, scaled, NT)
        va_sum = va_sum + mm(v, ac, NT)
        v_v[:, span(c)] = v
        p = mm(pair, uc, NN)
        g_v[c, :RANK, :n] = (SCALE * ratio) * (p[:RANK] + p[RANK:])
        g_v[c, RANK : RANK + 1, :n] = along
        g_v[c, RANK + 1 :, :] = jnp.zeros((PH - RANK - 1, PW), F32)
        g_v[c, RANK : RANK + 1, CW:] = jnp.zeros((1, PW - CW), F32)
    s_out[...] = s_sum
    gb = mm(s_sum.astype(BF16), tok[...], NN) - mm(va_sum.astype(BF16), b2t, NN)
    for c in range(NC):
        copies[c].wait()
        vm_sum = vm_sum + mm(v_v[:, span(c)], w[:, span(c)], NT)
    gb = SCALE * (gb - vm_sum)
    for c in range(NC):
        g_v[c, :RANK, CW:] = gb[:, 128 * c : 128 * (c + 1)]
    core = lax.rem(dp_place(), 2)
    for x in range(4):
        keep[x] = g_v[2 * x + core]
        send[x] = g_v[2 * x + 1 - core]


def third_kernel(zz, mag, s_ref, bt, u, w_h, o0, o1, o2, o3, acc, w, sems):
    copies = columns(w_h, w, sems)
    acc[...] = mm(s_ref[...].astype(BF16), bt[...] * BF16(SCALE), TN)
    for c in range(NC):
        n = WIDTHS[c]
        ratio = mag[c : c + 1, :n] / jnp.sqrt(zz[c, 0:1, :n] + EPS)
        scaled = (u[:, span(c)].astype(F32) * ratio).astype(BF16)
        copies[c].wait()
        acc[...] += mm(scaled, w[:, span(c)], NT)
    for d, o in enumerate((o0, o1, o2, o3)):
        part = lax.rem(lax.axis_index("col") + d, 4)
        o[...] = acc[:, pl.ds(pl.multiple_of(part * 256, 256), 256)]


def combine_kernel(y, zz, mag, pack, gb4):
    s = dp_place()
    total = (y[0] + y[1]) + (y[2] + y[3])
    mine = zz[s]
    normsq = mine[0:1] + EPS
    root = jnp.sqrt(normsq)
    ratio = mag[pl.ds(s, 1), :] / root
    along = total[RANK : RANK + 1, :CW]
    factor = (SCALE * ratio) * (along / normsq)
    for r in range(NC):
        rows = slice(4 * r, 4 * r + 4)
        pack[rows, :CW] = total[rows, :CW] - factor * zz[r, 2:6, :]
    pack[RANK : RANK + 1, :CW] = along / root
    pack[RANK + 1 :, :CW] = jnp.zeros((PH - RANK - 1, CW), F32)
    pack[:, CW:] = jnp.zeros((PH, PW - CW), F32)
    gb = total[:RANK, CW:]
    for i in range(4):
        gb4[i] = gb


def spread_kernel(pack, gb4, out):
    gb = (gb4[0] + gb4[1]) + (gb4[2] + gb4[3])
    for i in range(4):
        out[i] = pack[...]
        out[i, :RANK, CW:] = gb


def last_kernel(own, other, ga, gm, gb):
    even = dp_place() % 2 == 0
    for c in range(NC):
        mine = own if c % 2 == 0 else other
        theirs = other if c % 2 == 0 else own
        chunk = jnp.where(even, mine[c // 2], theirs[c // 2])
        ga[:, span(c)] = chunk[:RANK, : WIDTHS[c]]
        gm[span(c)] = chunk[RANK, : WIDTHS[c]]
        gb[:, 128 * c : 128 * (c + 1)] = chunk[:RANK, CW:]


def call(kernel, name, ins, outs, scratch=(), cost=None, limit=32):
    shapes = [
        pltpu.VMEM(*o) if isinstance(o[0], tuple) else jax.ShapeDtypeStruct(o, F32) for o in outs
    ]
    return pl.pallas_call(
        kernel,
        name=name,
        out_shape=shapes if len(shapes) > 1 else shapes[0],
        in_specs=ins,
        out_specs=[VMEM] * len(outs) if len(outs) > 1 else VMEM,
        scratch_shapes=list(scratch),
        cost_estimate=cost,
        compiler_params=pltpu.CompilerParams(vmem_limit_bytes=int(limit * (1 << 20))),
    )


def in_hbm(x):
    return pltpu.with_memory_space_constraint(x, pltpu.HBM)


COST = pl.CostEstimate(
    flops=4 * TOK * ROWS * COLS, bytes_accessed=10_000_000, transcendentals=COLS
)


def norms(tokens, bt, factor_a, weight, upstream):
    return call(
        first_kernel,
        "norms",
        [HBM, HBM, HBM, HBM, HBM],
        [
            ((NC, 8, CW), F32),
            ((TOK, ROWS), BF16),
            ((RANK, ROWS), BF16),
            ((RANK, COLS), BF16),
            ((TOK, COLS), BF16),
        ],
        (
            pltpu.VMEM((ROWS, COLS), BF16),
            pltpu.VMEM((ROWS, TOK), BF16),
            pltpu.VMEM((ROWS, RANK), BF16),
            pltpu.SemaphoreType.DMA((2, len(UNITS))),
            pltpu.SemaphoreType.DMA((3,)),
        ),
        COST,
        LIMIT,
    )(*(in_hbm(x) for x in (tokens, bt, factor_a, weight, upstream)))


def factors(zz, mag, tok, bt, a, u, weight):
    return call(
        second_kernel,
        "factors",
        [VMEM] * 6 + [HBM],
        [(4, PH, PW), (4, PH, PW), (RANK, TOK)],
        (
            pltpu.VMEM((NC, PH, PW), F32),
            pltpu.VMEM((RANK, TOK), F32),
            pltpu.VMEM((RANK, COLS), BF16),
            pltpu.VMEM((ROWS, COLS), BF16),
            pltpu.SemaphoreType.DMA((NC,)),
        ),
        COST,
    )(zz, mag, tok, bt, a, u, in_hbm(weight))


def tokens_grad(zz, mag, s_part, bt, u, weight):
    return call(
        third_kernel,
        "tokens_grad",
        [VMEM] * 5 + [HBM],
        [(TOK, 256)] * 4,
        (
            pltpu.VMEM((TOK, ROWS), F32),
            pltpu.VMEM((ROWS, COLS), BF16),
            pltpu.SemaphoreType.DMA((NC,)),
        ),
        COST,
    )(zz, mag, s_part, bt, u, in_hbm(weight))


def shards(tokens, upstream, weight, factor_b, factor_a, magnitude):
    mag = jnp.pad(magnitude, (0, NC * CW - COLS)).reshape(NC, CW)
    bt = factor_b.T
    part, tok, bt, a, u = norms(tokens, bt, factor_a, weight, upstream)
    z = jnp.sum(lax.all_to_all(part, "row", 0, 0, tiled=True), 0)
    zz = lax.all_to_all(jnp.broadcast_to(z[None], part.shape), "row", 0, 0, tiled=True)

    keep, send, s_part = factors(zz, mag, tok, bt, a, u, weight)
    halves = keep + lax.ppermute(send, "dp", CORE_FLIP)
    halves, s_part = lax.optimization_barrier((halves, s_part))
    y = lax.all_to_all(halves, "dp", 0, 0, tiled=True, axis_index_groups=X_GROUPS)
    o0, o1, o2, o3 = tokens_grad(zz, mag, s_part, bt, u, weight)

    pack, gb4 = call(
        combine_kernel, "combine", [VMEM, VMEM, VMEM], [(PH, PW), (4, RANK, 128)]
    )(y, zz, mag)
    gb4, o1, o2, o3 = lax.optimization_barrier((gb4, o1, o2, o3))
    gb4 = lax.all_to_all(gb4, "col", 0, 0, tiled=True)
    arrived = [
        lax.ppermute(o, "col", [(i, (i + d) % 4) for i in range(4)])
        for d, o in ((1, o1), (2, o2), (3, o3))
    ]
    first, third, gb4 = lax.optimization_barrier((arrived[0], arrived[2], gb4))
    arrived = [first, arrived[1], third]
    packs = call(spread_kernel, "spread", [VMEM, VMEM], [(4, PH, PW)])(pack, gb4)
    own = lax.all_to_all(packs, "dp", 0, 0, tiled=True, axis_index_groups=X_GROUPS)
    other = lax.ppermute(own, "dp", CORE_FLIP)
    grad_a, gm, gbt = call(
        last_kernel, "outputs", [VMEM, VMEM], [(RANK, COLS), (COLS,), (RANK, ROWS)]
    )(own, other)
    grad_tokens = ((o0 + arrived[0]) + (arrived[1] + arrived[2])).astype(BF16)
    return grad_tokens, gm, grad_a, gbt.T


def solution(mesh):
    placed = (
        P("dp", "row"),
        P("dp", "col"),
        P("row", "col"),
        P("row", None),
        P(None, "col"),
        P("col"),
    )
    return jax.shard_map(
        shards,
        mesh=mesh,
        in_specs=placed,
        out_specs=(P("dp", ("row", "col")), P("col"), P(None, "col"), P("row", None)),
        check_vma=False,
    )
```

```python
import jax
import jax.numpy as jnp
from jax import lax
from jax.experimental import pallas as pl
from jax.experimental.pallas import tpu as pltpu
from jax.sharding import PartitionSpec as P

SCALE = 2.0
EPS = 1e-06

TOK, ROWS, COLS, RANK = 256, 1024, 3712, 32
CW = 512
NC = 8
LIMIT = 28
DEPTH = 2
UNITS = [512] * 7 + [128]
WIDTHS = [min(CW, COLS - CW * c) for c in range(NC)]
PW = CW + 128
PH = 40
X_GROUPS = [[0, 2, 4, 6], [1, 3, 5, 7]]
CORE_FLIP = [(i, i ^ 1) for i in range(8)]
F32, BF16 = jnp.float32, jnp.bfloat16
NN = (((1,), (0,)), ((), ()))
NT = (((1,), (1,)), ((), ()))
TN = (((0,), (0,)), ((), ()))

VMEM = pl.BlockSpec(memory_space=pltpu.VMEM)
HBM = pl.BlockSpec(memory_space=pl.ANY)


def mm(a, b, dims):
    return lax.dot_general(a, b, dims, preferred_element_type=F32)


def dp_place():
    return lax.axis_index("dp")


def span(c):
    return pl.ds(CW * c, WIDTHS[c])


def first_kernel(tok_h, bt_h, a_h, w_h, u_h, out, tok, bt, a, u, w, tok_t, b_v, sems, small):
    firsts = [
        pltpu.make_async_copy(src, dst, small.at[i])
        for i, (src, dst) in enumerate(((tok_h, tok), (bt_h, bt), (a_h, a)))
    ]
    for copy in firsts:
        copy.start()
    units = [(sum(UNITS[:i]), n) for i, n in enumerate(UNITS)]
    copies = [
        [
            pltpu.make_async_copy(src.at[:, pl.ds(at, n)], dst.at[:, pl.ds(at, n)], sems.at[j, i])
            for j, (src, dst) in enumerate(((u_h, u), (w_h, w)))
        ]
        for i, (at, n) in enumerate(units)
    ]

    def begin(i):
        if i < len(units):
            copies[i][0].start()
            copies[i][1].start()

    for i in range(DEPTH):
        begin(i)
    out[NC - 1] = jnp.zeros((8, CW), F32)
    for copy in firsts:
        copy.wait()
    b2t = bt[...] * BF16(SCALE)
    tok_t[...] = tok[...].T
    b_v[...] = b2t.T
    low = mm(bt[...], tok[...], NT)
    gram = mm(bt[...], b2t, NT).astype(BF16)
    for r in range(NC):
        for i in range(4):
            lane = TOK * (i % 2)
            out[r, 6 + i // 2 : 7 + i // 2, lane : lane + TOK] = low[4 * r + i : 4 * r + i + 1]
    for i, (at, n) in enumerate(units):
        copies[i][0].wait()
        copies[i][1].wait()
        begin(i + DEPTH)
        here = pl.ds(at, n)
        merged = w[:, here].astype(F32) + mm(b_v[...], a[:, here], NN)
        outer = mm(tok_t[...], u[:, here], NN)
        squares = jnp.sum((merged * merged).reshape(ROWS // 8, 8, n), 0)
        products = jnp.sum((merged * outer).reshape(ROWS // 8, 8, n), 0)
        lo = at % CW
        out[at // CW, 0:1, lo : lo + n] = jnp.sum(squares, 0, keepdims=True)
        out[at // CW, 1:2, lo : lo + n] = jnp.sum(products, 0, keepdims=True)
    last = NC - 1

    def store(q, n):
        for r in range(NC):
            out[r, 2:6, :n] = q[4 * r : 4 * r + 4]
            if n < CW:
                out[r, 2:6, n:] = jnp.zeros((4, CW - n), F32)

    place = dp_place()

    @pl.when(place < last)
    def _():
        mine = pl.ds(pl.multiple_of(place * CW, CW), CW)
        store(mm(bt[...], w[:, mine], NN) + mm(gram, a[:, mine], NN), CW)

    @pl.when(place == last)
    def _():
        store(mm(bt[...], w[:, span(last)], NN) + mm(gram, a[:, span(last)], NN), WIDTHS[last])


def columns(src, dst, sems):
    copies = [
        pltpu.make_async_copy(src.at[:, span(c)], dst.at[:, span(c)], sems.at[c])
        for c in range(NC)
    ]
    for copy in copies:
        copy.start()
    return copies


def sum_kernel(parts, out):
    total = jnp.sum(parts[...], 0)
    for r in range(NC):
        out[r] = total


def add_kernel(a, b, out):
    out[...] = a[...] + b[...]


def second_kernel(zz, mag, tok, bt, a, u, w_h, keep, send, s_out, g_v, t_v, w, sems):
    copies = columns(w_h, w, sems)
    b2t = bt[...] * BF16(SCALE)
    for r in range(NC):
        for i in range(4):
            lane = TOK * (i % 2)
            t_v[4 * r + i : 4 * r + i + 1, :] = zz[r, 6 + i // 2 : 7 + i // 2, lane : lane + TOK]
    low = t_v[...]
    high = low.astype(BF16)
    pair = jnp.concatenate([high, (low - high.astype(F32)).astype(BF16)], 0)
    s_sum = jnp.zeros((RANK, TOK), F32)
    va_sum = jnp.zeros((RANK, RANK), F32)
    vm_sum = jnp.zeros((RANK, ROWS), F32)
    g_v[NC - 1] = jnp.zeros((PH, PW), F32)
    for c in range(NC):
        n = WIDTHS[c]
        uc, ac = u[:, span(c)], a[:, span(c)]
        normsq = zz[c, 0:1, :n] + EPS
        along = zz[c, 1:2, :n]
        ratio = mag[c : c + 1, :n] / jnp.sqrt(normsq)
        v = (ac.astype(F32) * (ratio * (along / normsq))).astype(BF16)
        scaled = (uc.astype(F32) * ratio).astype(BF16)
        s_sum = s_sum + mm(ac, scaled, NT)
        va_sum = va_sum + mm(v, ac, NT)
        copies[c].wait()
        vm_sum = vm_sum + mm(v, w[:, span(c)], NT)
        p = mm(pair, uc, NN)
        g_v[c, :RANK, :n] = (SCALE * ratio) * (p[:RANK] + p[RANK:])
        g_v[c, RANK : RANK + 1, :n] = along
        g_v[c, RANK + 1 :, :] = jnp.zeros((PH - RANK - 1, PW), F32)
        g_v[c, RANK : RANK + 1, CW:] = jnp.zeros((1, PW - CW), F32)
    s_out[...] = s_sum
    gb = mm(s_sum.astype(BF16), tok[...], NN) - mm(va_sum.astype(BF16), b2t, NN)
    gb = SCALE * (gb - vm_sum)
    for c in range(NC):
        g_v[c, :RANK, CW:] = gb[:, 128 * c : 128 * (c + 1)]
    core = lax.rem(dp_place(), 2)
    for x in range(4):
        keep[x] = g_v[2 * x + core]
        send[x] = g_v[2 * x + 1 - core]


def third_kernel(zz, mag, s_ref, bt, u, w_h, o0, o1, o2, o3, acc, w, sems):
    copies = columns(w_h, w, sems)
    acc[...] = mm(s_ref[...].astype(BF16), bt[...] * BF16(SCALE), TN)
    for c in range(NC):
        n = WIDTHS[c]
        ratio = mag[c : c + 1, :n] / jnp.sqrt(zz[c, 0:1, :n] + EPS)
        scaled = (u[:, span(c)].astype(F32) * ratio).astype(BF16)
        copies[c].wait()
        acc[...] += mm(scaled, w[:, span(c)], NT)
    for d, o in enumerate((o0, o1, o2, o3)):
        part = lax.rem(lax.axis_index("col") + d, 4)
        o[...] = acc[:, pl.ds(pl.multiple_of(part * 256, 256), 256)]


def combine_kernel(y, zz, mag, pack, gb):
    s = dp_place()
    total = (y[0] + y[1]) + (y[2] + y[3])
    mine = zz[s]
    normsq = mine[0:1] + EPS
    root = jnp.sqrt(normsq)
    ratio = mag[pl.ds(s, 1), :] / root
    along = total[RANK : RANK + 1, :CW]
    factor = (SCALE * ratio) * (along / normsq)
    for r in range(NC):
        rows = slice(4 * r, 4 * r + 4)
        pack[rows, :CW] = total[rows, :CW] - factor * zz[r, 2:6, :]
    pack[RANK : RANK + 1, :CW] = along / root
    pack[RANK + 1 :, :CW] = jnp.zeros((PH - RANK - 1, CW), F32)
    pack[:, CW:] = jnp.zeros((PH, PW - CW), F32)
    gb[...] = total[:RANK, CW:]


def spread_kernel(pack, g0, g1, g2, g3, out):
    gb = (g0[...] + g1[...]) + (g2[...] + g3[...])
    for i in range(4):
        out[i] = pack[...]
        out[i, :RANK, CW:] = gb


def last_kernel(own, other, ga, gm, gb):
    even = dp_place() % 2 == 0
    for c in range(NC):
        mine = own if c % 2 == 0 else other
        theirs = other if c % 2 == 0 else own
        chunk = jnp.where(even, mine[c // 2], theirs[c // 2])
        ga[:, span(c)] = chunk[:RANK, : WIDTHS[c]]
        gm[span(c)] = chunk[RANK, : WIDTHS[c]]
        gb[:, 128 * c : 128 * (c + 1)] = chunk[:RANK, CW:]


def call(kernel, name, ins, outs, scratch=(), cost=None, limit=32):
    shapes = [
        pltpu.VMEM(*o) if isinstance(o[0], tuple) else jax.ShapeDtypeStruct(o, F32) for o in outs
    ]
    return pl.pallas_call(
        kernel,
        name=name,
        out_shape=shapes if len(shapes) > 1 else shapes[0],
        in_specs=ins,
        out_specs=[VMEM] * len(outs) if len(outs) > 1 else VMEM,
        scratch_shapes=list(scratch),
        cost_estimate=cost,
        compiler_params=pltpu.CompilerParams(vmem_limit_bytes=int(limit * (1 << 20))),
    )


def in_hbm(x):
    return pltpu.with_memory_space_constraint(x, pltpu.HBM)


COST = pl.CostEstimate(
    flops=4 * TOK * ROWS * COLS, bytes_accessed=10_000_000, transcendentals=COLS
)


def norms(tokens, bt, factor_a, weight, upstream):
    return call(
        first_kernel,
        "norms",
        [HBM, HBM, HBM, HBM, HBM],
        [
            ((NC, 8, CW), F32),
            ((TOK, ROWS), BF16),
            ((RANK, ROWS), BF16),
            ((RANK, COLS), BF16),
            ((TOK, COLS), BF16),
        ],
        (
            pltpu.VMEM((ROWS, COLS), BF16),
            pltpu.VMEM((ROWS, TOK), BF16),
            pltpu.VMEM((ROWS, RANK), BF16),
            pltpu.SemaphoreType.DMA((2, len(UNITS))),
            pltpu.SemaphoreType.DMA((3,)),
        ),
        COST,
        LIMIT,
    )(*(in_hbm(x) for x in (tokens, bt, factor_a, weight, upstream)))


def factors(zz, mag, tok, bt, a, u, weight):
    return call(
        second_kernel,
        "factors",
        [VMEM] * 6 + [HBM],
        [(4, PH, PW), (4, PH, PW), (RANK, TOK)],
        (
            pltpu.VMEM((NC, PH, PW), F32),
            pltpu.VMEM((RANK, TOK), F32),
            pltpu.VMEM((ROWS, COLS), BF16),
            pltpu.SemaphoreType.DMA((NC,)),
        ),
        COST,
    )(zz, mag, tok, bt, a, u, in_hbm(weight))


def tokens_grad(zz, mag, s_part, bt, u, weight):
    return call(
        third_kernel,
        "tokens_grad",
        [VMEM] * 5 + [HBM],
        [(TOK, 256)] * 4,
        (
            pltpu.VMEM((TOK, ROWS), F32),
            pltpu.VMEM((ROWS, COLS), BF16),
            pltpu.SemaphoreType.DMA((NC,)),
        ),
        COST,
    )(zz, mag, s_part, bt, u, in_hbm(weight))


def from_col(x, d):
    return lax.ppermute(x, "col", [(i, (i + d) % 4) for i in range(4)])


def shards(tokens, upstream, weight, factor_b, factor_a, magnitude):
    mag = jnp.pad(magnitude, (0, NC * CW - COLS)).reshape(NC, CW)
    bt = factor_b.T
    part, tok, bt, a, u = norms(tokens, bt, factor_a, weight, upstream)
    parts = lax.all_to_all(part, "row", 0, 0, tiled=True)
    sums = call(sum_kernel, "sum", [VMEM], [((NC, 8, CW), F32)])(parts)
    zz = lax.all_to_all(sums, "row", 0, 0, tiled=True)

    keep, send, s_part = factors(zz, mag, tok, bt, a, u, weight)
    other = lax.ppermute(send, "dp", CORE_FLIP)
    halves = call(add_kernel, "add", [VMEM, VMEM], [((4, PH, PW), F32)])(keep, other)
    halves, s_part = lax.optimization_barrier((halves, s_part))
    y = lax.all_to_all(halves, "dp", 0, 0, tiled=True, axis_index_groups=X_GROUPS)
    o0, o1, o2, o3 = tokens_grad(zz, mag, s_part, bt, u, weight)

    pack, gb = call(
        combine_kernel, "combine", [VMEM, VMEM, VMEM], [(PH, PW), (RANK, 128)]
    )(y, zz, mag)
    gb, o1, o2, o3 = lax.optimization_barrier((gb, o1, o2, o3))
    gbs = [gb] + [from_col(gb, d) for d in (1, 2, 3)]
    arrived = [from_col(o, d) for d, o in ((1, o1), (2, o2), (3, o3))]
    first, third, gbs[0] = lax.optimization_barrier((arrived[0], arrived[2], gbs[0]))
    arrived = [first, arrived[1], third]
    packs = call(spread_kernel, "spread", [VMEM] * 5, [((4, PH, PW), F32)])(pack, *gbs)
    own = lax.all_to_all(packs, "dp", 0, 0, tiled=True, axis_index_groups=X_GROUPS)
    other = lax.ppermute(own, "dp", CORE_FLIP)
    grad_a, gm, gbt = call(
        last_kernel, "outputs", [VMEM, VMEM], [(RANK, COLS), (COLS,), (RANK, ROWS)]
    )(own, other)
    grad_tokens = ((o0 + arrived[0]) + (arrived[1] + arrived[2])).astype(BF16)
    return grad_tokens, gm, grad_a, gbt.T


def solution(mesh):
    placed = (
        P("dp", "row"),
        P("dp", "col"),
        P("row", "col"),
        P("row", None),
        P(None, "col"),
        P("col"),
    )
    return jax.shard_map(
        shards,
        mesh=mesh,
        in_specs=placed,
        out_specs=(P("dp", ("row", "col")), P("col"), P(None, "col"), P("row", None)),
        check_vma=False,
    )
```

```python
import jax
import jax.numpy as jnp
from jax import lax
from jax.experimental import pallas as pl
from jax.experimental.pallas import tpu as pltpu
from jax.sharding import PartitionSpec as P

SCALE = 2.0
EPS = 1e-06

TOK, ROWS, COLS, RANK = 256, 1024, 3712, 32
CW = 512
NC = 8
LIMIT = 28
DEPTH = 2
UNITS = [512] * 7 + [128]
WIDTHS = [min(CW, COLS - CW * c) for c in range(NC)]
PW = CW + 128
PH = 40
CORE_FLIP = [(i, i ^ 1) for i in range(8)]
F32, BF16 = jnp.float32, jnp.bfloat16
NN = (((1,), (0,)), ((), ()))
NT = (((1,), (1,)), ((), ()))
TN = (((0,), (0,)), ((), ()))

VMEM = pl.BlockSpec(memory_space=pltpu.VMEM)
HBM = pl.BlockSpec(memory_space=pl.ANY)


def mm(a, b, dims):
    return lax.dot_general(a, b, dims, preferred_element_type=F32)


def dp_place():
    return lax.axis_index("dp")


def span(c):
    return pl.ds(CW * c, WIDTHS[c])


def first_kernel(tok_h, bt_h, a_h, w_h, u_h, out, tok, bt, a, u, w, tok_t, b_v, sems, small):
    firsts = [
        pltpu.make_async_copy(src, dst, small.at[i])
        for i, (src, dst) in enumerate(((tok_h, tok), (bt_h, bt), (a_h, a)))
    ]
    for copy in firsts:
        copy.start()
    units = [(sum(UNITS[:i]), n) for i, n in enumerate(UNITS)]
    copies = [
        [
            pltpu.make_async_copy(src.at[:, pl.ds(at, n)], dst.at[:, pl.ds(at, n)], sems.at[j, i])
            for j, (src, dst) in enumerate(((u_h, u), (w_h, w)))
        ]
        for i, (at, n) in enumerate(units)
    ]

    def begin(i):
        if i < len(units):
            copies[i][0].start()
            copies[i][1].start()

    for i in range(DEPTH):
        begin(i)
    out[NC - 1] = jnp.zeros((8, CW), F32)
    for copy in firsts:
        copy.wait()
    b2t = bt[...] * BF16(SCALE)
    tok_t[...] = tok[...].T
    b_v[...] = b2t.T
    low = mm(bt[...], tok[...], NT)
    gram = mm(bt[...], b2t, NT).astype(BF16)
    for r in range(NC):
        for i in range(4):
            lane = TOK * (i % 2)
            out[r, 6 + i // 2 : 7 + i // 2, lane : lane + TOK] = low[4 * r + i : 4 * r + i + 1]
    for i, (at, n) in enumerate(units):
        copies[i][0].wait()
        copies[i][1].wait()
        begin(i + DEPTH)
        here = pl.ds(at, n)
        merged = w[:, here].astype(F32) + mm(b_v[...], a[:, here], NN)
        outer = mm(tok_t[...], u[:, here], NN)
        squares = jnp.sum((merged * merged).reshape(ROWS // 8, 8, n), 0)
        products = jnp.sum((merged * outer).reshape(ROWS // 8, 8, n), 0)
        lo = at % CW
        out[at // CW, 0:1, lo : lo + n] = jnp.sum(squares, 0, keepdims=True)
        out[at // CW, 1:2, lo : lo + n] = jnp.sum(products, 0, keepdims=True)
    last = NC - 1

    def store(q, n):
        for r in range(NC):
            out[r, 2:6, :n] = q[4 * r : 4 * r + 4]
            if n < CW:
                out[r, 2:6, n:] = jnp.zeros((4, CW - n), F32)

    place = dp_place()

    @pl.when(place < last)
    def _():
        mine = pl.ds(pl.multiple_of(place * CW, CW), CW)
        store(mm(bt[...], w[:, mine], NN) + mm(gram, a[:, mine], NN), CW)

    @pl.when(place == last)
    def _():
        store(mm(bt[...], w[:, span(last)], NN) + mm(gram, a[:, span(last)], NN), WIDTHS[last])


def columns(src, dst, sems):
    copies = [
        pltpu.make_async_copy(src.at[:, span(c)], dst.at[:, span(c)], sems.at[c])
        for c in range(NC)
    ]
    for copy in copies:
        copy.start()
    return copies


def sum_kernel(parts, out):
    total = jnp.sum(parts[...], 0)
    for r in range(NC):
        out[r] = total


def add_kernel(a, b, *outs):
    x = dp_place() // 2
    for d, out in enumerate(outs):
        part = lax.rem(x + d, 4)
        out[...] = a[part] + b[part]


def second_kernel(zz, mag, tok, bt, a, u, w_h, keep, send, s_out, g_v, t_v, w, sems):
    copies = columns(w_h, w, sems)
    b2t = bt[...] * BF16(SCALE)
    for r in range(NC):
        for i in range(4):
            lane = TOK * (i % 2)
            t_v[4 * r + i : 4 * r + i + 1, :] = zz[r, 6 + i // 2 : 7 + i // 2, lane : lane + TOK]
    low = t_v[...]
    high = low.astype(BF16)
    pair = jnp.concatenate([high, (low - high.astype(F32)).astype(BF16)], 0)
    s_sum = jnp.zeros((RANK, TOK), F32)
    va_sum = jnp.zeros((RANK, RANK), F32)
    vm_sum = jnp.zeros((RANK, ROWS), F32)
    g_v[NC - 1] = jnp.zeros((PH, PW), F32)
    for c in range(NC):
        n = WIDTHS[c]
        uc, ac = u[:, span(c)], a[:, span(c)]
        normsq = zz[c, 0:1, :n] + EPS
        along = zz[c, 1:2, :n]
        ratio = mag[c : c + 1, :n] / jnp.sqrt(normsq)
        v = (ac.astype(F32) * (ratio * (along / normsq))).astype(BF16)
        scaled = (uc.astype(F32) * ratio).astype(BF16)
        s_sum = s_sum + mm(ac, scaled, NT)
        va_sum = va_sum + mm(v, ac, NT)
        copies[c].wait()
        vm_sum = vm_sum + mm(v, w[:, span(c)], NT)
        p = mm(pair, uc, NN)
        g_v[c, :RANK, :n] = (SCALE * ratio) * (p[:RANK] + p[RANK:])
        g_v[c, RANK : RANK + 1, :n] = along
        g_v[c, RANK + 1 :, :] = jnp.zeros((PH - RANK - 1, PW), F32)
        g_v[c, RANK : RANK + 1, CW:] = jnp.zeros((1, PW - CW), F32)
    s_out[...] = s_sum
    gb = mm(s_sum.astype(BF16), tok[...], NN) - mm(va_sum.astype(BF16), b2t, NN)
    gb = SCALE * (gb - vm_sum)
    for c in range(NC):
        g_v[c, :RANK, CW:] = gb[:, 128 * c : 128 * (c + 1)]
    core = lax.rem(dp_place(), 2)
    for x in range(4):
        keep[x] = g_v[2 * x + core]
        send[x] = g_v[2 * x + 1 - core]


def third_kernel(zz, mag, s_ref, bt_h, u, w_h, o0, o1, o2, o3, acc, w, bt, sems, small):
    copies = columns(w_h, w, sems)
    last = pltpu.make_async_copy(bt_h, bt, small.at[0])
    last.start()
    acc[...] = jnp.zeros((TOK, ROWS), F32)
    for c in range(NC):
        n = WIDTHS[c]
        ratio = mag[c : c + 1, :n] / jnp.sqrt(zz[c, 0:1, :n] + EPS)
        scaled = (u[:, span(c)].astype(F32) * ratio).astype(BF16)
        copies[c].wait()
        acc[...] += mm(scaled, w[:, span(c)], NT)
    last.wait()
    acc[...] += mm(s_ref[...].astype(BF16), bt[...] * BF16(SCALE), TN)
    for d, o in enumerate((o0, o1, o2, o3)):
        part = lax.rem(lax.axis_index("col") + d, 4)
        o[...] = acc[:, pl.ds(pl.multiple_of(part * 256, 256), 256)]


def combine_kernel(y0, y1, y2, y3, zz, mag, pack, gb):
    s = dp_place()
    total = (y0[...] + y1[...]) + (y2[...] + y3[...])
    mine = zz[s]
    normsq = mine[0:1] + EPS
    root = jnp.sqrt(normsq)
    ratio = mag[pl.ds(s, 1), :] / root
    along = total[RANK : RANK + 1, :CW]
    factor = (SCALE * ratio) * (along / normsq)
    for r in range(NC):
        rows = slice(4 * r, 4 * r + 4)
        pack[rows, :CW] = total[rows, :CW] - factor * zz[r, 2:6, :]
    pack[RANK : RANK + 1, :CW] = along / root
    pack[RANK + 1 :, :CW] = jnp.zeros((PH - RANK - 1, CW), F32)
    pack[:, CW:] = jnp.zeros((PH, PW - CW), F32)
    gb[...] = total[:RANK, CW:]


def finish_kernel(pack, g0, g1, g2, g3, out):
    out[...] = pack[...]
    out[:RANK, CW:] = (g0[...] + g1[...]) + (g2[...] + g3[...])


def last_kernel(p0, p1, p2, p3, f0, f1, f2, f3, ga, gm, gb, both):
    place = dp_place()
    core = lax.rem(place, 2)
    for d, (own, other) in enumerate(((p0, f0), (p1, f1), (p2, f2), (p3, f3))):
        x = lax.rem(place // 2 + 4 - d, 4)
        both[2 * x + core] = own[...]
        both[2 * x + 1 - core] = other[...]
    for c in range(NC):
        ga[:, span(c)] = both[c, :RANK, : WIDTHS[c]]
        gm[span(c)] = both[c, RANK, : WIDTHS[c]]
        gb[:, 128 * c : 128 * (c + 1)] = both[c, :RANK, CW:]


def call(kernel, name, ins, outs, scratch=(), cost=None, limit=32):
    shapes = [
        pltpu.VMEM(*o) if isinstance(o[0], tuple) else jax.ShapeDtypeStruct(o, F32) for o in outs
    ]
    return pl.pallas_call(
        kernel,
        name=name,
        out_shape=shapes if len(shapes) > 1 else shapes[0],
        in_specs=ins,
        out_specs=[VMEM] * len(outs) if len(outs) > 1 else VMEM,
        scratch_shapes=list(scratch),
        cost_estimate=cost,
        compiler_params=pltpu.CompilerParams(vmem_limit_bytes=int(limit * (1 << 20))),
    )


def in_hbm(x):
    return pltpu.with_memory_space_constraint(x, pltpu.HBM)


COST = pl.CostEstimate(
    flops=4 * TOK * ROWS * COLS, bytes_accessed=10_000_000, transcendentals=COLS
)


def norms(tokens, bt, factor_a, weight, upstream):
    return call(
        first_kernel,
        "norms",
        [HBM, HBM, HBM, HBM, HBM],
        [
            ((NC, 8, CW), F32),
            ((TOK, ROWS), BF16),
            ((RANK, ROWS), BF16),
            ((RANK, COLS), BF16),
            ((TOK, COLS), BF16),
        ],
        (
            pltpu.VMEM((ROWS, COLS), BF16),
            pltpu.VMEM((ROWS, TOK), BF16),
            pltpu.VMEM((ROWS, RANK), BF16),
            pltpu.SemaphoreType.DMA((2, len(UNITS))),
            pltpu.SemaphoreType.DMA((3,)),
        ),
        COST,
        LIMIT,
    )(*(in_hbm(x) for x in (tokens, bt, factor_a, weight, upstream)))


def factors(zz, mag, tok, bt, a, u, weight):
    return call(
        second_kernel,
        "factors",
        [VMEM] * 6 + [HBM],
        [(4, PH, PW), (4, PH, PW), (RANK, TOK)],
        (
            pltpu.VMEM((NC, PH, PW), F32),
            pltpu.VMEM((RANK, TOK), F32),
            pltpu.VMEM((ROWS, COLS), BF16),
            pltpu.SemaphoreType.DMA((NC,)),
        ),
        COST,
    )(zz, mag, tok, bt, a, u, in_hbm(weight))


def tokens_grad(zz, mag, s_part, bt, u, weight):
    return call(
        third_kernel,
        "tokens_grad",
        [VMEM] * 3 + [HBM, VMEM, HBM],
        [(TOK, 256)] * 4,
        (
            pltpu.VMEM((TOK, ROWS), F32),
            pltpu.VMEM((ROWS, COLS), BF16),
            pltpu.VMEM((RANK, ROWS), BF16),
            pltpu.SemaphoreType.DMA((NC,)),
            pltpu.SemaphoreType.DMA((1,)),
        ),
        COST,
    )(zz, mag, s_part, in_hbm(bt), u, in_hbm(weight))


def along_x(x, d):
    return lax.ppermute(x, "dp", [(i, (i + 2 * d) % 8) for i in range(8)])


def from_col(x, d):
    return lax.ppermute(x, "col", [(i, (i + d) % 4) for i in range(4)])


def shards(tokens, upstream, weight, factor_b, factor_a, magnitude):
    mag = jnp.pad(magnitude, (0, NC * CW - COLS)).reshape(NC, CW)
    bt = factor_b.T
    part, tok, bt_near, a, u = norms(tokens, bt, factor_a, weight, upstream)
    parts = lax.all_to_all(part, "row", 0, 0, tiled=True)
    sums = call(sum_kernel, "sum", [VMEM], [((NC, 8, CW), F32)])(parts)
    zz = lax.all_to_all(sums, "row", 0, 0, tiled=True)

    keep, send, s_part = factors(zz, mag, tok, bt_near, a, u, weight)
    other = lax.ppermute(send, "dp", CORE_FLIP)
    halves = call(add_kernel, "add", [VMEM, VMEM], [(PH, PW)] * 4)(keep, other)
    halves, s_part = lax.optimization_barrier((halves, s_part))
    y = [halves[0]] + [along_x(halves[d], d) for d in (1, 2, 3)]
    o0, o1, o2, o3 = tokens_grad(zz, mag, s_part, bt, u, weight)

    pack, gb = call(
        combine_kernel, "combine", [VMEM] * 6, [(PH, PW), (RANK, 128)]
    )(*y, zz, mag)
    gb, o1, o2, o3 = lax.optimization_barrier((gb, o1, o2, o3))
    gbs = [gb] + [from_col(gb, d) for d in (1, 2, 3)]
    first, third, gbs[0] = lax.optimization_barrier((from_col(o1, 1), from_col(o3, 3), gbs[0]))
    pack = call(finish_kernel, "finish", [VMEM] * 5, [(PH, PW)])(pack, *gbs)
    pack, o2 = lax.optimization_barrier((pack, o2))
    arrived = [first, from_col(o2, 2), third]
    own = [pack] + [along_x(pack, d) for d in (1, 2, 3)]
    other = [lax.ppermute(p, "dp", CORE_FLIP) for p in own]
    grad_a, gm, gbt = call(
        last_kernel,
        "outputs",
        [VMEM] * 8,
        [(RANK, COLS), (COLS,), (RANK, ROWS)],
        (pltpu.VMEM((NC, PH, PW), F32),),
    )(*own, *other)
    grad_tokens = ((o0 + arrived[0]) + (arrived[1] + arrived[2])).astype(BF16)
    return grad_tokens, gm, grad_a, gbt.T


def solution(mesh):
    placed = (
        P("dp", "row"),
        P("dp", "col"),
        P("row", "col"),
        P("row", None),
        P(None, "col"),
        P("col"),
    )
    return jax.shard_map(
        shards,
        mesh=mesh,
        in_specs=placed,
        out_specs=(P("dp", ("row", "col")), P("col"), P(None, "col"), P("row", None)),
        check_vma=False,
    )
```

```python
import jax
import jax.numpy as jnp
from jax import lax
from jax.experimental import pallas as pl
from jax.experimental.pallas import tpu as pltpu
from jax.sharding import PartitionSpec as P

SCALE = 2.0
EPS = 1e-06

TOK, ROWS, COLS, RANK = 256, 1024, 3712, 32
CW = 512
NC = 8
LIMIT = 28
DEPTH = 2
UNITS = [512] * 7 + [128]
WIDTHS = [min(CW, COLS - CW * c) for c in range(NC)]
PW = CW + 128
PH = 40
CORE_FLIP = [(i, i ^ 1) for i in range(8)]
F32, BF16 = jnp.float32, jnp.bfloat16
NN = (((1,), (0,)), ((), ()))
NT = (((1,), (1,)), ((), ()))
TN = (((0,), (0,)), ((), ()))

VMEM = pl.BlockSpec(memory_space=pltpu.VMEM)
HBM = pl.BlockSpec(memory_space=pl.ANY)


def mm(a, b, dims):
    return lax.dot_general(a, b, dims, preferred_element_type=F32)


def dp_place():
    return lax.axis_index("dp")


def span(c):
    return pl.ds(CW * c, WIDTHS[c])


def first_kernel(tok_h, bt_h, a_h, w_h, u_h, out, tok, bt, a, u, w, tok_t, b_v, sems, small):
    firsts = [
        pltpu.make_async_copy(src, dst, small.at[i])
        for i, (src, dst) in enumerate(((tok_h, tok), (bt_h, bt), (a_h, a)))
    ]
    for copy in firsts:
        copy.start()
    units = [(sum(UNITS[:i]), n) for i, n in enumerate(UNITS)]
    copies = [
        [
            pltpu.make_async_copy(src.at[:, pl.ds(at, n)], dst.at[:, pl.ds(at, n)], sems.at[j, i])
            for j, (src, dst) in enumerate(((u_h, u), (w_h, w)))
        ]
        for i, (at, n) in enumerate(units)
    ]

    def begin(i):
        if i < len(units):
            copies[i][0].start()
            copies[i][1].start()

    for i in range(DEPTH):
        begin(i)
    out[NC - 1] = jnp.zeros((8, CW), F32)
    for copy in firsts:
        copy.wait()
    b2t = bt[...] * BF16(SCALE)
    tok_t[...] = tok[...].T
    b_v[...] = b2t.T
    low = mm(bt[...], tok[...], NT)
    gram = mm(bt[...], b2t, NT).astype(BF16)
    for r in range(NC):
        for i in range(4):
            lane = TOK * (i % 2)
            out[r, 6 + i // 2 : 7 + i // 2, lane : lane + TOK] = low[4 * r + i : 4 * r + i + 1]
    for i, (at, n) in enumerate(units):
        copies[i][0].wait()
        copies[i][1].wait()
        begin(i + DEPTH)
        here = pl.ds(at, n)
        merged = w[:, here].astype(F32) + mm(b_v[...], a[:, here], NN)
        outer = mm(tok_t[...], u[:, here], NN)
        squares = jnp.sum((merged * merged).reshape(ROWS // 8, 8, n), 0)
        products = jnp.sum((merged * outer).reshape(ROWS // 8, 8, n), 0)
        lo = at % CW
        out[at // CW, 0:1, lo : lo + n] = jnp.sum(squares, 0, keepdims=True)
        out[at // CW, 1:2, lo : lo + n] = jnp.sum(products, 0, keepdims=True)
    last = NC - 1

    def store(q, n):
        for r in range(NC):
            out[r, 2:6, :n] = q[4 * r : 4 * r + 4]
            if n < CW:
                out[r, 2:6, n:] = jnp.zeros((4, CW - n), F32)

    place = dp_place()

    @pl.when(place < last)
    def _():
        mine = pl.ds(pl.multiple_of(place * CW, CW), CW)
        store(mm(bt[...], w[:, mine], NN) + mm(gram, a[:, mine], NN), CW)

    @pl.when(place == last)
    def _():
        store(mm(bt[...], w[:, span(last)], NN) + mm(gram, a[:, span(last)], NN), WIDTHS[last])


def columns(src, dst, sems):
    copies = [
        pltpu.make_async_copy(src.at[:, span(c)], dst.at[:, span(c)], sems.at[c])
        for c in range(NC)
    ]
    for copy in copies:
        copy.start()
    return copies


def sum_kernel(parts, out):
    total = jnp.sum(parts[...], 0)
    for r in range(NC):
        out[r] = total


def add_kernel(a, b, *outs):
    x = dp_place() // 2
    for d, out in enumerate(outs):
        part = lax.rem(x + d, 4)
        out[...] = a[part] + b[part]


def second_kernel(zz, mag, tok, bt, a, u, w_h, keep, send, s_out, g_v, t_v, w, sems):
    copies = columns(w_h, w, sems)
    b2t = bt[...] * BF16(SCALE)
    for r in range(NC):
        for i in range(4):
            lane = TOK * (i % 2)
            t_v[4 * r + i : 4 * r + i + 1, :] = zz[r, 6 + i // 2 : 7 + i // 2, lane : lane + TOK]
    low = t_v[...]
    high = low.astype(BF16)
    pair = jnp.concatenate([high, (low - high.astype(F32)).astype(BF16)], 0)
    s_sum = jnp.zeros((RANK, TOK), F32)
    va_sum = jnp.zeros((RANK, RANK), F32)
    vm_sum = jnp.zeros((RANK, ROWS), F32)
    g_v[NC - 1] = jnp.zeros((PH, PW), F32)
    for c in range(NC):
        n = WIDTHS[c]
        uc, ac = u[:, span(c)], a[:, span(c)]
        normsq = zz[c, 0:1, :n] + EPS
        along = zz[c, 1:2, :n]
        ratio = mag[c : c + 1, :n] / jnp.sqrt(normsq)
        v = (ac.astype(F32) * (ratio * (along / normsq))).astype(BF16)
        scaled = (uc.astype(F32) * ratio).astype(BF16)
        s_sum = s_sum + mm(ac, scaled, NT)
        va_sum = va_sum + mm(v, ac, NT)
        copies[c].wait()
        vm_sum = vm_sum + mm(v, w[:, span(c)], NT)
        p = mm(pair, uc, NN)
        g_v[c, :RANK, :n] = (SCALE * ratio) * (p[:RANK] + p[RANK:])
        g_v[c, RANK : RANK + 1, :n] = along
        g_v[c, RANK + 1 :, :] = jnp.zeros((PH - RANK - 1, PW), F32)
        g_v[c, RANK : RANK + 1, CW:] = jnp.zeros((1, PW - CW), F32)
    s_out[...] = s_sum
    gb = mm(s_sum.astype(BF16), tok[...], NN) - mm(va_sum.astype(BF16), b2t, NN)
    gb = SCALE * (gb - vm_sum)
    for c in range(NC):
        g_v[c, :RANK, CW:] = gb[:, 128 * c : 128 * (c + 1)]
    core = lax.rem(dp_place(), 2)
    for x in range(4):
        keep[x] = g_v[2 * x + core]
        send[x] = g_v[2 * x + 1 - core]


def third_kernel(zz, mag, s_ref, bt_h, u, w_h, o0, o1, o3, o2a, o2b, acc, w, bt, sems, small):
    copies = columns(w_h, w, sems)
    last = pltpu.make_async_copy(bt_h, bt, small.at[0])
    last.start()
    acc[...] = jnp.zeros((TOK, ROWS), F32)
    for c in range(NC):
        n = WIDTHS[c]
        ratio = mag[c : c + 1, :n] / jnp.sqrt(zz[c, 0:1, :n] + EPS)
        scaled = (u[:, span(c)].astype(F32) * ratio).astype(BF16)
        copies[c].wait()
        acc[...] += mm(scaled, w[:, span(c)], NT)
    last.wait()
    acc[...] += mm(s_ref[...].astype(BF16), bt[...] * BF16(SCALE), TN)
    half = TOK // 2
    for d, rows, o in (
        (0, slice(0, TOK), o0),
        (1, slice(0, TOK), o1),
        (3, slice(0, TOK), o3),
        (2, slice(0, half), o2a),
        (2, slice(half, TOK), o2b),
    ):
        part = lax.rem(lax.axis_index("col") + d, 4)
        o[...] = acc[rows, pl.ds(pl.multiple_of(part * 256, 256), 256)]


def combine_kernel(y0, y1, y2, y3, zz, mag, pack, gb):
    s = dp_place()
    total = (y0[...] + y1[...]) + (y2[...] + y3[...])
    mine = zz[s]
    normsq = mine[0:1] + EPS
    root = jnp.sqrt(normsq)
    ratio = mag[pl.ds(s, 1), :] / root
    along = total[RANK : RANK + 1, :CW]
    factor = (SCALE * ratio) * (along / normsq)
    for r in range(NC):
        rows = slice(4 * r, 4 * r + 4)
        pack[rows, :CW] = total[rows, :CW] - factor * zz[r, 2:6, :]
    pack[RANK : RANK + 1, :CW] = along / root
    pack[RANK + 1 :, :CW] = jnp.zeros((PH - RANK - 1, CW), F32)
    pack[:, CW:] = jnp.zeros((PH, PW - CW), F32)
    gb[...] = total[:RANK, CW:]


def finish_kernel(pack, g0, g1, g2, g3, o1, o3, ra, rb, out, s1, s3):
    half = TOK // 2
    s1[:half] = o1[:half] + ra[...]
    s1[half:] = o1[half:]
    s3[:half] = o3[:half]
    s3[half:] = o3[half:] + rb[...]
    out[...] = pack[...]
    out[:RANK, CW:] = (g0[...] + g1[...]) + (g2[...] + g3[...])


def last_kernel(p0, p1, p2, p3, f0, f1, f2, f3, ga, gm, gb, both):
    place = dp_place()
    core = lax.rem(place, 2)
    for d, (own, other) in enumerate(((p0, f0), (p1, f1), (p2, f2), (p3, f3))):
        x = lax.rem(place // 2 + 4 - d, 4)
        both[2 * x + core] = own[...]
        both[2 * x + 1 - core] = other[...]
    for c in range(NC):
        ga[:, span(c)] = both[c, :RANK, : WIDTHS[c]]
        gm[span(c)] = both[c, RANK, : WIDTHS[c]]
        gb[:, 128 * c : 128 * (c + 1)] = both[c, :RANK, CW:]


def call(kernel, name, ins, outs, scratch=(), cost=None, limit=32):
    shapes = [
        pltpu.VMEM(*o) if isinstance(o[0], tuple) else jax.ShapeDtypeStruct(o, F32) for o in outs
    ]
    return pl.pallas_call(
        kernel,
        name=name,
        out_shape=shapes if len(shapes) > 1 else shapes[0],
        in_specs=ins,
        out_specs=[VMEM] * len(outs) if len(outs) > 1 else VMEM,
        scratch_shapes=list(scratch),
        cost_estimate=cost,
        compiler_params=pltpu.CompilerParams(vmem_limit_bytes=int(limit * (1 << 20))),
    )


def in_hbm(x):
    return pltpu.with_memory_space_constraint(x, pltpu.HBM)


COST = pl.CostEstimate(
    flops=4 * TOK * ROWS * COLS, bytes_accessed=10_000_000, transcendentals=COLS
)


def norms(tokens, bt, factor_a, weight, upstream):
    return call(
        first_kernel,
        "norms",
        [HBM, HBM, HBM, HBM, HBM],
        [
            ((NC, 8, CW), F32),
            ((TOK, ROWS), BF16),
            ((RANK, ROWS), BF16),
            ((RANK, COLS), BF16),
            ((TOK, COLS), BF16),
        ],
        (
            pltpu.VMEM((ROWS, COLS), BF16),
            pltpu.VMEM((ROWS, TOK), BF16),
            pltpu.VMEM((ROWS, RANK), BF16),
            pltpu.SemaphoreType.DMA((2, len(UNITS))),
            pltpu.SemaphoreType.DMA((3,)),
        ),
        COST,
        LIMIT,
    )(*(in_hbm(x) for x in (tokens, bt, factor_a, weight, upstream)))


def factors(zz, mag, tok, bt, a, u, weight):
    return call(
        second_kernel,
        "factors",
        [VMEM] * 6 + [HBM],
        [(4, PH, PW), (4, PH, PW), (RANK, TOK)],
        (
            pltpu.VMEM((NC, PH, PW), F32),
            pltpu.VMEM((RANK, TOK), F32),
            pltpu.VMEM((ROWS, COLS), BF16),
            pltpu.SemaphoreType.DMA((NC,)),
        ),
        COST,
    )(zz, mag, tok, bt, a, u, in_hbm(weight))


def tokens_grad(zz, mag, s_part, bt, u, weight):
    return call(
        third_kernel,
        "tokens_grad",
        [VMEM] * 3 + [HBM, VMEM, HBM],
        [(TOK, 256)] * 3 + [(TOK // 2, 256)] * 2,
        (
            pltpu.VMEM((TOK, ROWS), F32),
            pltpu.VMEM((ROWS, COLS), BF16),
            pltpu.VMEM((RANK, ROWS), BF16),
            pltpu.SemaphoreType.DMA((NC,)),
            pltpu.SemaphoreType.DMA((1,)),
        ),
        COST,
    )(zz, mag, s_part, in_hbm(bt), u, in_hbm(weight))


def along_x(x, d):
    return lax.ppermute(x, "dp", [(i, (i + 2 * d) % 8) for i in range(8)])


def from_col(x, d):
    return lax.ppermute(x, "col", [(i, (i + d) % 4) for i in range(4)])


def shards(tokens, upstream, weight, factor_b, factor_a, magnitude):
    mag = jnp.pad(magnitude, (0, NC * CW - COLS)).reshape(NC, CW)
    bt = factor_b.T
    part, tok, bt_near, a, u = norms(tokens, bt, factor_a, weight, upstream)
    parts = lax.all_to_all(part, "row", 0, 0, tiled=True)
    sums = call(sum_kernel, "sum", [VMEM], [((NC, 8, CW), F32)])(parts)
    zz = lax.all_to_all(sums, "row", 0, 0, tiled=True)

    keep, send, s_part = factors(zz, mag, tok, bt_near, a, u, weight)
    other = lax.ppermute(send, "dp", CORE_FLIP)
    halves = call(add_kernel, "add", [VMEM, VMEM], [(PH, PW)] * 4)(keep, other)
    halves, s_part = lax.optimization_barrier((halves, s_part))
    y = [halves[0]] + [along_x(halves[d], d) for d in (1, 2, 3)]
    o0, o1, o3, o2a, o2b = tokens_grad(zz, mag, s_part, bt, u, weight)

    pack, gb = call(
        combine_kernel, "combine", [VMEM] * 6, [(PH, PW), (RANK, 128)]
    )(*y, zz, mag)
    gb, o2a, o2b = lax.optimization_barrier((gb, o2a, o2b))
    gbs = [gb] + [from_col(gb, d) for d in (1, 2, 3)]
    ra, rb = from_col(o2a, 1), from_col(o2b, 3)
    pack, s1, s3 = call(
        finish_kernel, "finish", [VMEM] * 9, [(PH, PW), (TOK, 256), (TOK, 256)]
    )(pack, *gbs, o1, o3, ra, rb)
    arrived = from_col(s1, 1), from_col(s3, 3)
    own = [pack] + [along_x(pack, d) for d in (1, 2, 3)]
    other = [lax.ppermute(p, "dp", CORE_FLIP) for p in own]
    grad_a, gm, gbt = call(
        last_kernel,
        "outputs",
        [VMEM] * 8,
        [(RANK, COLS), (COLS,), (RANK, ROWS)],
        (pltpu.VMEM((NC, PH, PW), F32),),
    )(*own, *other)
    grad_tokens = (o0 + (arrived[0] + arrived[1])).astype(BF16)
    return grad_tokens, gm, grad_a, gbt.T


def solution(mesh):
    placed = (
        P("dp", "row"),
        P("dp", "col"),
        P("row", "col"),
        P("row", None),
        P(None, "col"),
        P("col"),
    )
    return jax.shard_map(
        shards,
        mesh=mesh,
        in_specs=placed,
        out_specs=(P("dp", ("row", "col")), P("col"), P(None, "col"), P("row", None)),
        check_vma=False,
    )
```

```python
import jax
import jax.numpy as jnp
from jax import lax
from jax.experimental import pallas as pl
from jax.experimental.pallas import tpu as pltpu
from jax.sharding import PartitionSpec as P

SCALE = 2.0
EPS = 1e-06

TOK, ROWS, COLS, RANK = 256, 1024, 3712, 32
CW = 512
NC = 8
LIMIT = 28
DEPTH = 2
UNITS = [512] * 7 + [128]
WIDTHS = [min(CW, COLS - CW * c) for c in range(NC)]
PW = CW + 128
PH = 40
CORE_FLIP = [(i, i ^ 1) for i in range(8)]
F32, BF16 = jnp.float32, jnp.bfloat16
NN = (((1,), (0,)), ((), ()))
NT = (((1,), (1,)), ((), ()))
TN = (((0,), (0,)), ((), ()))

VMEM = pl.BlockSpec(memory_space=pltpu.VMEM)
HBM = pl.BlockSpec(memory_space=pl.ANY)


def mm(a, b, dims):
    return lax.dot_general(a, b, dims, preferred_element_type=F32)


def dp_place():
    return lax.axis_index("dp")


def span(c):
    return pl.ds(CW * c, WIDTHS[c])


def first_kernel(tok_h, bt_h, a_h, w_h, u_h, out, tok, bt, a, u, w, tok_t, b_v, sems, small):
    firsts = [
        pltpu.make_async_copy(src, dst, small.at[i])
        for i, (src, dst) in enumerate(((tok_h, tok), (bt_h, bt), (a_h, a)))
    ]
    for copy in firsts:
        copy.start()
    units = [(sum(UNITS[:i]), n) for i, n in enumerate(UNITS)]
    copies = [
        [
            pltpu.make_async_copy(src.at[:, pl.ds(at, n)], dst.at[:, pl.ds(at, n)], sems.at[j, i])
            for j, (src, dst) in enumerate(((u_h, u), (w_h, w)))
        ]
        for i, (at, n) in enumerate(units)
    ]

    def begin(i):
        if i < len(units):
            copies[i][0].start()
            copies[i][1].start()

    for i in range(DEPTH):
        begin(i)
    out[NC - 1] = jnp.zeros((8, CW), F32)
    for copy in firsts:
        copy.wait()
    b2t = bt[...] * BF16(SCALE)
    tok_t[...] = tok[...].T
    b_v[...] = b2t.T
    low = mm(bt[...], tok[...], NT)
    gram = mm(bt[...], b2t, NT).astype(BF16)
    for r in range(NC):
        for i in range(4):
            lane = TOK * (i % 2)
            out[r, 6 + i // 2 : 7 + i // 2, lane : lane + TOK] = low[4 * r + i : 4 * r + i + 1]
    for i, (at, n) in enumerate(units):
        copies[i][0].wait()
        copies[i][1].wait()
        begin(i + DEPTH)
        here = pl.ds(at, n)
        merged = w[:, here].astype(F32) + mm(b_v[...], a[:, here], NN)
        outer = mm(tok_t[...], u[:, here], NN)
        squares = jnp.sum((merged * merged).reshape(ROWS // 8, 8, n), 0)
        products = jnp.sum((merged * outer).reshape(ROWS // 8, 8, n), 0)
        lo = at % CW
        out[at // CW, 0:1, lo : lo + n] = jnp.sum(squares, 0, keepdims=True)
        out[at // CW, 1:2, lo : lo + n] = jnp.sum(products, 0, keepdims=True)
    last = NC - 1

    def store(q, n):
        for r in range(NC):
            out[r, 2:6, :n] = q[4 * r : 4 * r + 4]
            if n < CW:
                out[r, 2:6, n:] = jnp.zeros((4, CW - n), F32)

    place = dp_place()

    @pl.when(place < last)
    def _():
        mine = pl.ds(pl.multiple_of(place * CW, CW), CW)
        store(mm(bt[...], w[:, mine], NN) + mm(gram, a[:, mine], NN), CW)

    @pl.when(place == last)
    def _():
        store(mm(bt[...], w[:, span(last)], NN) + mm(gram, a[:, span(last)], NN), WIDTHS[last])


def columns(src, dst, sems):
    copies = [
        pltpu.make_async_copy(src.at[:, span(c)], dst.at[:, span(c)], sems.at[c])
        for c in range(NC)
    ]
    for copy in copies:
        copy.start()
    return copies


def sum_kernel(parts, out):
    total = jnp.sum(parts[...], 0)
    for r in range(NC):
        out[r] = total


def add_kernel(a, b, *outs):
    x = dp_place() // 2
    for d, out in enumerate(outs):
        part = lax.rem(x + d, 4)
        out[...] = a[part] + b[part]


def second_kernel(zz, mag, tok, bt, a, u, w_h, keep, send, s_out, g_v, t_v, w, sems):
    copies = columns(w_h, w, sems)
    b2t = bt[...] * BF16(SCALE)
    for r in range(NC):
        for i in range(4):
            lane = TOK * (i % 2)
            t_v[4 * r + i : 4 * r + i + 1, :] = zz[r, 6 + i // 2 : 7 + i // 2, lane : lane + TOK]
    low = t_v[...]
    high = low.astype(BF16)
    pair = jnp.concatenate([high, (low - high.astype(F32)).astype(BF16)], 0)
    s_sum = jnp.zeros((RANK, TOK), F32)
    va_sum = jnp.zeros((RANK, RANK), F32)
    vm_sum = jnp.zeros((RANK, ROWS), F32)
    g_v[NC - 1] = jnp.zeros((PH, PW), F32)
    for c in range(NC):
        n = WIDTHS[c]
        uc, ac = u[:, span(c)], a[:, span(c)]
        normsq = zz[c, 0:1, :n] + EPS
        along = zz[c, 1:2, :n]
        ratio = mag[c : c + 1, :n] / jnp.sqrt(normsq)
        v = (ac.astype(F32) * (ratio * (along / normsq))).astype(BF16)
        scaled = (uc.astype(F32) * ratio).astype(BF16)
        s_sum = s_sum + mm(ac, scaled, NT)
        va_sum = va_sum + mm(v, ac, NT)
        copies[c].wait()
        vm_sum = vm_sum + mm(v, w[:, span(c)], NT)
        p = mm(pair, uc, NN)
        g_v[c, :RANK, :n] = (SCALE * ratio) * (p[:RANK] + p[RANK:])
        g_v[c, RANK : RANK + 1, :n] = along
        g_v[c, RANK + 1 :, :] = jnp.zeros((PH - RANK - 1, PW), F32)
        g_v[c, RANK : RANK + 1, CW:] = jnp.zeros((1, PW - CW), F32)
    s_out[...] = s_sum
    gb = mm(s_sum.astype(BF16), tok[...], NN) - mm(va_sum.astype(BF16), b2t, NN)
    gb = SCALE * (gb - vm_sum)
    for c in range(NC):
        g_v[c, :RANK, CW:] = gb[:, 128 * c : 128 * (c + 1)]
    core = lax.rem(dp_place(), 2)
    for x in range(4):
        keep[x] = g_v[2 * x + core]
        send[x] = g_v[2 * x + 1 - core]


def third_kernel(zz, mag, s_ref, bt_h, u, w_h, o0, o1, o3, o2a, o2b, acc, w, bt, sems, small):
    copies = columns(w_h, w, sems)
    last = pltpu.make_async_copy(bt_h, bt, small.at[0])
    last.start()
    acc[...] = jnp.zeros((TOK, ROWS), F32)
    for c in range(NC):
        n = WIDTHS[c]
        ratio = mag[c : c + 1, :n] / jnp.sqrt(zz[c, 0:1, :n] + EPS)
        scaled = (u[:, span(c)].astype(F32) * ratio).astype(BF16)
        copies[c].wait()
        acc[...] += mm(scaled, w[:, span(c)], NT)
    last.wait()
    acc[...] += mm(s_ref[...].astype(BF16), bt[...] * BF16(SCALE), TN)
    half = TOK // 2
    for d, rows, o in (
        (0, slice(0, TOK), o0),
        (1, slice(0, TOK), o1),
        (3, slice(0, TOK), o3),
        (2, slice(0, half), o2a),
        (2, slice(half, TOK), o2b),
    ):
        part = lax.rem(lax.axis_index("col") + d, 4)
        o[...] = acc[rows, pl.ds(pl.multiple_of(part * 256, 256), 256)]


def combine_kernel(y0, y1, y2, y3, zz, mag, pack, gb):
    s = dp_place()
    total = (y0[...] + y1[...]) + (y2[...] + y3[...])
    mine = zz[s]
    normsq = mine[0:1] + EPS
    root = jnp.sqrt(normsq)
    ratio = mag[pl.ds(s, 1), :] / root
    along = total[RANK : RANK + 1, :CW]
    factor = (SCALE * ratio) * (along / normsq)
    for r in range(NC):
        rows = slice(4 * r, 4 * r + 4)
        pack[rows, :CW] = total[rows, :CW] - factor * zz[r, 2:6, :]
    pack[RANK : RANK + 1, :CW] = along / root
    pack[RANK + 1 :, :CW] = jnp.zeros((PH - RANK - 1, CW), F32)
    pack[:, CW:] = jnp.zeros((PH, PW - CW), F32)
    gb[...] = total[:RANK, CW:]


def finish_kernel(pack, g0, g1, g2, g3, o1, o3, ra, rb, out, s1, s3):
    half = TOK // 2
    s1[:half] = o1[:half] + ra[...]
    s1[half:] = o1[half:]
    s3[:half] = o3[:half]
    s3[half:] = o3[half:] + rb[...]
    out[...] = pack[...]
    out[:RANK, CW:] = (g0[...] + g1[...]) + (g2[...] + g3[...])


def last_kernel(p0, p1, p2, p3, f0, f1, f2, f3, ga, gm, gb, both):
    place = dp_place()
    core = lax.rem(place, 2)
    for d, (own, other) in enumerate(((p0, f0), (p1, f1), (p2, f2), (p3, f3))):
        x = lax.rem(place // 2 + 4 - d, 4)
        both[2 * x + core] = own[...]
        both[2 * x + 1 - core] = other[...]
    for c in range(NC):
        ga[:, span(c)] = both[c, :RANK, : WIDTHS[c]]
        gm[span(c)] = both[c, RANK, : WIDTHS[c]]
        gb[:, 128 * c : 128 * (c + 1)] = both[c, :RANK, CW:]


def call(kernel, name, ins, outs, scratch=(), cost=None, limit=32):
    shapes = [
        pltpu.VMEM(*o) if isinstance(o[0], tuple) else jax.ShapeDtypeStruct(o, F32) for o in outs
    ]
    return pl.pallas_call(
        kernel,
        name=name,
        out_shape=shapes if len(shapes) > 1 else shapes[0],
        in_specs=ins,
        out_specs=[VMEM] * len(outs) if len(outs) > 1 else VMEM,
        scratch_shapes=list(scratch),
        cost_estimate=cost,
        compiler_params=pltpu.CompilerParams(vmem_limit_bytes=int(limit * (1 << 20))),
    )


def in_hbm(x):
    return pltpu.with_memory_space_constraint(x, pltpu.HBM)


COST = pl.CostEstimate(
    flops=4 * TOK * ROWS * COLS, bytes_accessed=10_000_000, transcendentals=COLS
)


def norms(tokens, bt, factor_a, weight, upstream):
    return call(
        first_kernel,
        "norms",
        [HBM, HBM, HBM, HBM, HBM],
        [
            ((NC, 8, CW), F32),
            ((TOK, ROWS), BF16),
            ((RANK, ROWS), BF16),
            ((RANK, COLS), BF16),
            ((TOK, COLS), BF16),
        ],
        (
            pltpu.VMEM((ROWS, COLS), BF16),
            pltpu.VMEM((ROWS, TOK), BF16),
            pltpu.VMEM((ROWS, RANK), BF16),
            pltpu.SemaphoreType.DMA((2, len(UNITS))),
            pltpu.SemaphoreType.DMA((3,)),
        ),
        COST,
        LIMIT,
    )(*(in_hbm(x) for x in (tokens, bt, factor_a, weight, upstream)))


def factors(zz, mag, tok, bt, a, u, weight):
    return call(
        second_kernel,
        "factors",
        [VMEM] * 6 + [HBM],
        [(4, PH, PW), (4, PH, PW), (RANK, TOK)],
        (
            pltpu.VMEM((NC, PH, PW), F32),
            pltpu.VMEM((RANK, TOK), F32),
            pltpu.VMEM((ROWS, COLS), BF16),
            pltpu.SemaphoreType.DMA((NC,)),
        ),
        COST,
    )(zz, mag, tok, bt, a, u, in_hbm(weight))


def tokens_grad(zz, mag, s_part, bt, u, weight):
    return call(
        third_kernel,
        "tokens_grad",
        [VMEM] * 3 + [HBM, VMEM, HBM],
        [(TOK, 256)] * 3 + [(TOK // 2, 256)] * 2,
        (
            pltpu.VMEM((TOK, ROWS), F32),
            pltpu.VMEM((ROWS, COLS), BF16),
            pltpu.VMEM((RANK, ROWS), BF16),
            pltpu.SemaphoreType.DMA((NC,)),
            pltpu.SemaphoreType.DMA((1,)),
        ),
        COST,
    )(zz, mag, s_part, in_hbm(bt), u, in_hbm(weight))


def along_x(x, d):
    return lax.ppermute(x, "dp", [(i, (i + 2 * d) % 8) for i in range(8)])


def from_col(x, d):
    return lax.ppermute(x, "col", [(i, (i + d) % 4) for i in range(4)])


def shards(tokens, upstream, weight, factor_b, factor_a, magnitude):
    mag = jnp.pad(magnitude, (0, NC * CW - COLS)).reshape(NC, CW)
    bt = factor_b.T
    part, tok, bt_near, a, u = norms(tokens, bt, factor_a, weight, upstream)
    parts = lax.all_to_all(part, "row", 0, 0, tiled=True)
    sums = call(sum_kernel, "sum", [VMEM], [((NC, 8, CW), F32)])(parts)
    zz = lax.all_to_all(sums, "row", 0, 0, tiled=True)

    keep, send, s_part = factors(zz, mag, tok, bt_near, a, u, weight)
    other = lax.ppermute(send, "dp", CORE_FLIP)
    halves = call(add_kernel, "add", [VMEM, VMEM], [(PH, PW)] * 4)(keep, other)
    halves, s_part = lax.optimization_barrier((halves, s_part))
    y = [halves[0]] + [along_x(halves[d], d) for d in (1, 2, 3)]
    o0, o1, o3, o2a, o2b = tokens_grad(zz, mag, s_part, bt, u, weight)

    pack, gb = call(
        combine_kernel, "combine", [VMEM] * 6, [(PH, PW), (RANK, 128)]
    )(*y, zz, mag)
    gb, o2a, o2b = lax.optimization_barrier((gb, o2a, o2b))
    gbs = [gb] + [from_col(gb, d) for d in (1, 2, 3)]
    ra, rb = from_col(o2a, 1), from_col(o2b, 3)
    pack, s1, s3 = call(
        finish_kernel, "finish", [VMEM] * 9, [(PH, PW), (TOK, 256), (TOK, 256)]
    )(pack, *gbs, o1, o3, ra, rb)
    own = [pack] + [along_x(pack, d) for d in (1, 2, 3)]
    own, s1, s3 = lax.optimization_barrier((own, s1, s3))
    arrived = from_col(s1, 1), from_col(s3, 3)
    other = [lax.ppermute(p, "dp", CORE_FLIP) for p in own]
    grad_a, gm, gbt = call(
        last_kernel,
        "outputs",
        [VMEM] * 8,
        [(RANK, COLS), (COLS,), (RANK, ROWS)],
        (pltpu.VMEM((NC, PH, PW), F32),),
    )(*own, *other)
    grad_tokens = (o0 + (arrived[0] + arrived[1])).astype(BF16)
    return grad_tokens, gm, grad_a, gbt.T


def solution(mesh):
    placed = (
        P("dp", "row"),
        P("dp", "col"),
        P("row", "col"),
        P("row", None),
        P(None, "col"),
        P("col"),
    )
    return jax.shard_map(
        shards,
        mesh=mesh,
        in_specs=placed,
        out_specs=(P("dp", ("row", "col")), P("col"), P(None, "col"), P("row", None)),
        check_vma=False,
    )
```
